128 devices in a mesh: blk: 8 (over z, y_lo), grp: 16 (over y_hi, x, core).
Axes of the slice: x: 4, y: 4 (y_hi: 2, y_lo: 2; y = y_hi * 2 + y_lo), z: 4, core: 2. Of those that a mesh axis runs over, the one named last changes fastest.
Arguments:
- student: bfloat16 [16384, 1024], P(('blk', 'grp')), may hold values from -6 to 6
- teacher: bfloat16 [16384, 4096], P(('blk', 'grp')), may hold values from -6 to 6
Outputs:
- student_grad: float32 [16384, 1024], P(('blk', 'grp'))
The draws below stay inside these ranges and needn't reach their ends.
All inputs are finite; a program needn't handle non-finite values.
Results may differ from the reference program's by a relative error of at most 0.0085.
Values may be sent and summed in bfloat16 or wider, within the bound.
No kernel may reach another device: no remote copies, remote signals or barrier semaphores. Data moves between devices by JAX's collectives and lax.ppermute only.
A program may use at most 192 MiB of HBM per device.

```python
import math
import jax
import jax.numpy as jnp
from jax import lax

DS = 1024
DT = 4096
TEXTS = 16384


def steps_of(key, dims, cuts, low, largest):
    level, own = 1.0, jax.random.fold_in(key, 6)
    for axis_at, blocks in cuts:
        draws = jnp.exp(jax.random.uniform(jax.random.fold_in(own, axis_at), (blocks,), jnp.float32, low / len(cuts), largest / len(cuts)))
        level = level * jnp.repeat(draws, dims[axis_at] // blocks).reshape([-1 if axis == axis_at else 1 for axis in range(len(dims))])
    return level


def normal_values(own_key, dims, scale, bound, shards=(), kind=jnp.bfloat16):
    values = scale * jax.random.normal(own_key, dims, jnp.float32)
    if shards:
        values = values * steps_of(own_key, dims, shards, -0.22, 0.18)
    return jnp.clip(values, -bound, bound).astype(kind)


def setup_inputs(seed: int = 0) -> dict:
    arg_keys = jax.random.split(jax.random.key(seed), 3)
    return {
        "student": normal_values(arg_keys[0], (TEXTS, DS), 1.0, 6.0, ((0, 128),)),
        "teacher": normal_values(arg_keys[1], (TEXTS, DT), 1.0, 6.0, ((0, 128),)),
    }


def unit_rows(values):
    wide = values.astype(jnp.float32)
    recip = 1.0 / jnp.sqrt(lax.optimization_barrier(jnp.sum(wide * wide, axis=1, keepdims=True)) + 1e-06)
    return (wide * recip, recip)

def reference(student, teacher):
    unit_f, recip = unit_rows(student)
    unit_s = unit_f.astype(jnp.bfloat16)
    teach_f, teach_r = unit_rows(teacher)
    unit_t = teach_f.astype(jnp.bfloat16)
    total = unit_s.shape[0]
    scale_s = math.sqrt(unit_s.shape[1])
    scale_t = math.sqrt(unit_t.shape[1])
    coef = 4.0 * unit_s.shape[1] / math.sqrt(total)
    stride = math.gcd(total, 1024)
    wide_s = unit_s.astype(jnp.float32)
    wide_t = unit_t.astype(jnp.float32)

    def one_block(index):
        start = (index * stride).astype(jnp.int32)
        rows_s = lax.dynamic_slice_in_dim(wide_s, start, stride, 0)
        rows_t = lax.dynamic_slice_in_dim(wide_t, start, stride, 0)
        squash_s = jnp.tanh(scale_s * jnp.dot(rows_s, wide_s.T))
        squash_t = jnp.tanh(scale_t * jnp.dot(rows_t, wide_t.T))
        weight = ((squash_s - squash_t) * scale_s * (1.0 - squash_s * squash_s)).astype(jnp.bfloat16)
        return jnp.dot(weight.astype(jnp.float32), wide_s)
    parts = lax.map(one_block, jnp.arange(total // stride, dtype=jnp.int32))
    dunit = coef * parts.reshape(total, unit_s.shape[1])
    inner = lax.optimization_barrier(jnp.sum(dunit * unit_f, axis=1, keepdims=True))
    return recip * (dunit - inner * unit_f)
```

```python
import functools
import itertools
import math

import jax
import jax.numpy as jnp
from jax import lax
from jax.experimental import pallas as pl
from jax.experimental.pallas import tpu as pltpu
from jax.sharding import PartitionSpec as P

ROWS = 128
DS, DT = 1024, 4096
WIDE = DS + DT
HALF = WIDE // 2
SCALE_S, SCALE_T = math.sqrt(DS), math.sqrt(DT)

LAYOUT_1 = ["000s", "000o", "001o", "003o", "030o", "300o", "300s", "010o", "010s"]
GROUPS_1 = [("000", [["000o"], ["001o"]]), ("300", [["000o", "001o", "003o", "030o"]]),
            ("010", [["000o", "001o", "003o", "030o", "300o"]])]
LAYOUT_2 = ["000s", "000o", "010o", "010s", "300o", "300s", "200o", "200s",
            "030o", "003o", "001o", "002o", "031o", "033o", "110o", "110s"]
GROUPS_2 = [("010", [["002o", "031o"]]), ("000", [["002o"], ["200o"]]), ("300", [["002o", "031o", "033o", "110o"]]),
            ("200", [["001o", "002o", "031o", "033o"]]), ("110", [["030o", "003o", "001o", "002o", "031o", "033o"]])]
LAYOUT_3 = ["032o", "032s", "010o", "300o", "110o", "200o", "210o", "210s", "030o", "031o"]
GROUPS_3 = [("032", [["010o", "300o", "110o", "200o", "210o"]]), ("210", [["030o", "031o"]])]


def offset(name):
    return tuple(int(t) for t in name[:3])


def fetch(block, distance, flip=False):
    dx, dy, dz = distance
    pairs = []
    for z, low, high, x, core in itertools.product(range(4), range(2), range(2), range(4), range(2)):
        y = (2 * high + low + dy) % 4
        source = ((((z + dz) % 4 * 2 + y % 2) * 2 + y // 2) * 4 + (x + dx) % 4) * 2 + (core ^ int(flip))
        target = (((z * 2 + low) * 2 + high) * 4 + x) * 2 + core
        pairs.append((source, target))
    return lax.ppermute(block, ("blk", "grp"), pairs)


def swap(block):
    return fetch(block, (0, 0, 0), True)


def give(block, name):
    return fetch(block, tuple(-t for t in offset(name)), name[3] == "s")


def unit_kernel(student, teacher, out):
    for source, first, width in ((student, 0, DS), (teacher, DS, DT)):
        wide = source[...].astype(jnp.float32)
        recip = 1.0 / jnp.sqrt(jnp.sum(wide * wide, axis=1, keepdims=True) + 1e-06)
        out[:, first : first + width] = (wide * recip).astype(jnp.bfloat16)


def unit_rows(student, teacher):
    return pl.pallas_call(
        unit_kernel,
        out_shape=jax.ShapeDtypeStruct((ROWS, WIDE), jnp.bfloat16),
        in_specs=[pl.BlockSpec(memory_space=pltpu.VMEM)] * 2,
        out_specs=pl.BlockSpec(memory_space=pltpu.VMEM),
        compiler_params=pltpu.CompilerParams(vmem_limit_bytes=16 << 20),
        name="unit_rows",
    )(student, teacher)


def involution(one, two):
    return all((2 * (s - t)) % 4 == 0 for s, t in zip(offset(one), offset(two)))


def phase_kernel(layout, groups, pieces, starts, adds, outs, *refs):
    at = {name: i * ROWS for i, name in enumerate(layout)}
    refs = list(refs)
    block_refs = [refs.pop(0) for _ in pieces]
    start_refs = [refs.pop(0) for _ in starts]
    add_ref = refs.pop(0) if adds else None
    out_refs = [refs.pop(0) for _ in outs]
    held, sums, acc_s, acc_t, weight, sems = refs[:6]
    added = refs[6] if adds else None
    copies = {}
    number = 0

    def begin(key, source, target):
        nonlocal number
        copy = pltpu.make_async_copy(source, target, sems.at[number])
        copy.start()
        copies.setdefault(key, []).append(copy)
        number += 1

    for (name, first), ref in zip(pieces, block_refs):
        begin(name, ref, held.at[pl.ds(at[name], ROWS), pl.ds(first, ref.shape[1])])
    touched = set()
    for names, ref in zip(starts, start_refs):
        for i, name in enumerate(names):
            if name is not None:
                begin("+" + name, ref.at[pl.ds(i * ROWS, ROWS), :], sums.at[pl.ds(at[name], ROWS), :])
                touched.add(name)
    if adds:
        begin("adds", add_ref, added)

    def ready(key):
        for copy in copies.pop(key, []):
            copy.wait()

    def put(names, value):
        first = at[names[0]]
        for i, name in enumerate(names):
            ready("+" + name)
            rows = pl.ds(first + i * ROWS, ROWS)
            part = value[i * ROWS : (i + 1) * ROWS]
            if name in touched:
                sums[rows, :] += part
            else:
                sums[rows, :] = part
                touched.add(name)

    nt = (((1,), (1,)), ((), ()))
    tn = (((0,), (0,)), ((), ()))
    for a, runs in groups:
        halves = sorted([a + "o", a + "s"], key=at.get)
        both = pl.ds(at[halves[0]], 2 * ROWS)
        for run in runs:
            for name in halves + run:
                ready(name)
            many = len(run) * ROWS
            rows = pl.ds(at[run[0]], many)
            part = pl.ds(0, many)
            acc_s[part, :] = lax.dot_general(
                held[rows, pl.ds(0, DS)], held[both, pl.ds(0, DS)], nt, preferred_element_type=jnp.float32
            )
            acc_t[part, :] = lax.dot_general(
                held[rows, pl.ds(DS, 1024)], held[both, pl.ds(DS, 1024)], nt, preferred_element_type=jnp.float32
            )

            @pl.loop(1, DT // 1024)
            def _(step):
                columns = pl.ds(pl.multiple_of(DS + step * 1024, 1024), 1024)
                acc_t[part, :] += lax.dot_general(
                    held[rows, columns], held[both, columns], nt, preferred_element_type=jnp.float32
                )

            for i, name in enumerate(run):
                tile = pl.ds(i * ROWS, ROWS)
                squash_s = jnp.tanh(SCALE_S * acc_s[tile, :])
                squash_t = jnp.tanh(SCALE_T * acc_t[tile, :])
                value = (squash_s - squash_t) * SCALE_S * (1.0 - squash_s * squash_s)
                if name[:3] != a and involution(a, name):
                    value = 0.5 * value
                weight[tile, :] = value.astype(jnp.bfloat16)
            put(run, jnp.dot(weight[part, :], held[both, pl.ds(0, DS)], preferred_element_type=jnp.float32))
            if run[0][:3] != a:
                put(halves, lax.dot_general(
                    weight[part, :], held[rows, pl.ds(0, DS)], tn, preferred_element_type=jnp.float32
                ))
    for key in list(copies):
        ready(key)
    for names, ref in zip(outs, out_refs):
        for i, name in enumerate(names):
            value = sums[pl.ds(at[name], ROWS), :]
            if name in adds:
                value = value + added[pl.ds(adds.index(name) * ROWS, ROWS), :].astype(jnp.float32)
            ref[pl.ds(i * ROWS, ROWS), :] = value.astype(ref.dtype)


def phase(name, layout, groups, blocks, starts, adds, outs):
    pairs = sum(len(run) for _, runs in groups for run in runs)
    most = max(len(run) for _, runs in groups for run in runs) * ROWS
    copies = len(blocks) + sum(sum(n is not None for n in names) for names, _ in starts) + 1
    shapes = [jax.ShapeDtypeStruct((len(names) * ROWS, DS), kind) for names, kind in outs]
    scratch = [
        pltpu.VMEM((len(layout) * ROWS, WIDE), jnp.bfloat16),
        pltpu.VMEM((len(layout) * ROWS, DS), jnp.float32),
        pltpu.VMEM((most, 2 * ROWS), jnp.float32),
        pltpu.VMEM((most, 2 * ROWS), jnp.float32),
        pltpu.VMEM((most, 2 * ROWS), jnp.bfloat16),
        pltpu.SemaphoreType.DMA((copies,)),
    ]
    operands = [array for _, _, array in blocks] + [array for _, array in starts]
    if adds:
        operands.append(adds[1])
        scratch.append(pltpu.VMEM(adds[1].shape, adds[1].dtype))
    return pl.pallas_call(
        functools.partial(
            phase_kernel, layout, groups, [(n, f) for n, f, _ in blocks], [names for names, _ in starts],
            adds[0] if adds else [], [names for names, _ in outs],
        ),
        out_shape=shapes,
        in_specs=[pl.BlockSpec(memory_space=pl.ANY)] * len(operands),
        out_specs=[pl.BlockSpec(memory_space=pltpu.VMEM)] * len(shapes),
        scratch_shapes=scratch,
        compiler_params=pltpu.CompilerParams(vmem_limit_bytes=56 << 20),
        cost_estimate=pl.CostEstimate(
            flops=pairs * 2 * ROWS * 2 * ROWS * (WIDE + 2 * DS) * 2,
            bytes_accessed=sum(x.size * x.dtype.itemsize for x in operands), transcendentals=0,
        ),
        name=name,
    )(*operands)


def local(student, teacher):
    own = unit_rows(student, teacher)
    f32, bf16 = jnp.float32, jnp.bfloat16
    got = {"000o": own, "000s": swap(own)}
    for name in ("010o", "300o", "001o", "003o", "030o"):
        got[name] = fetch(own, offset(name))
    for a in ("010", "300"):
        got[a + "s"] = swap(got[a + "o"])
    got["110o"] = fetch(got["010o"], (1, 0, 0))
    got["200o"] = fetch(got["300o"], (3, 0, 0))
    got["002o"] = fetch(got["003o"], (0, 0, 3))
    got["031o"] = fetch(got["030o"], (0, 0, 1))
    got["033o"] = fetch(got["003o"], (0, 3, 0))

    rows = lambda layout: [(name, 0, got[name]) for name in layout if name in got]
    names_1 = ["000s", "000o", "001o", "003o", "030o", "300o", "300s", "010o", "010s"]
    (sums_1,) = phase("phase_1", LAYOUT_1, GROUPS_1, rows(LAYOUT_1), [], None, [(names_1, f32)])

    for a in ("110", "200"):
        got[a + "s"] = swap(got[a + "o"])
    late = {
        ("032o", 0): fetch(got["031o"][:, :HALF], (0, 0, 1)),
        ("032o", HALF): fetch(got["033o"][:, HALF:], (0, 0, 3)),
        ("210o", 0): fetch(got["200o"][:, :HALF], (0, 1, 0)),
        ("210o", HALF): fetch(got["110o"][:, HALF:], (1, 0, 0)),
    }
    names_s = ["000s", "010s", "300s", "110s", "200s"]
    names_2 = ["010o", "300o", "110o", "200o", "030o", "031o"]
    early = ["001o", "003o", "002o", "033o"]
    siblings, sums_2, home, *done = phase(
        "phase_2", LAYOUT_2, GROUPS_2, rows(LAYOUT_2), [(names_1, sums_1)], None,
        [(names_s, bf16), (names_2, f32), (["000o"], f32)] + [([name], bf16) for name in early],
    )
    siblings = swap(siblings)
    back = [give(value, name) for name, value in zip(early, done)]

    for (name, first), array in list(late.items()):
        late[name[:3] + "s", first] = swap(array)
    last = ["032o", "032s", "210o", "210s", "110o", "200o", "031o", "010o", "300o", "030o"]
    done = phase(
        "phase_3", LAYOUT_3, GROUPS_3, rows(LAYOUT_3) + [(name, first, array) for (name, first), array in late.items()],
        [(names_2, sums_2)], (["none", "010o", "300o", "110o", "200o"], siblings),
        [([name], bf16) for name in last],
    )
    back += [give(value, name) for name, value in zip(last, done)]

    summed = home + siblings[:ROWS].astype(f32)
    for value in back:
        summed = summed + value.astype(f32)
    wide = student.astype(f32)
    recip = 1.0 / jnp.sqrt(jnp.sum(wide * wide, axis=1, keepdims=True) + 1e-06)
    unit_f = wide * recip
    dunit = (4.0 * DS / math.sqrt(16384)) * summed
    inner = jnp.sum(dunit * unit_f, axis=1, keepdims=True)
    return recip * (dunit - inner * unit_f)


def solution(mesh):
    spec = P(("blk", "grp"), None)
    return jax.shard_map(local, mesh=mesh, in_specs=(spec, spec), out_specs=spec, check_vma=False)
```

```python
import functools
import itertools
import math

import jax
import jax.numpy as jnp
from jax import lax
from jax.experimental import pallas as pl
from jax.experimental.pallas import tpu as pltpu
from jax.sharding import PartitionSpec as P

ROWS = 128
DS, DT = 1024, 4096
WIDE = DS + DT
HALF = WIDE // 2
PM = 2
SCALE_S, SCALE_T = math.sqrt(DS), math.sqrt(DT)

LAYOUT_1 = ["000s", "000o", "001o", "003o", "030o", "300o", "300s", "010o", "010s"]
GROUPS_1 = [("000", [["000o"], ["001o"]]), ("300", [["000o", "001o", "003o", "030o"]]),
            ("010", [["000o", "001o", "003o", "030o", "300o"]])]
LAYOUT_2 = ["000s", "000o", "010o", "010s", "300o", "300s", "200o", "200s",
            "030o", "003o", "001o", "002o", "031o", "033o", "110o", "110s"]
GROUPS_2 = [("000", [["002o"], ["200o"]]), ("010", [["002o", "031o"]]), ("300", [["002o", "031o", "033o", "110o"]]),
            ("200", [["001o", "002o", "031o", "033o"]]), ("110", [["030o", "003o", "001o", "002o", "031o", "033o"]])]
LAYOUT_3 = ["032o", "032s", "010o", "300o", "110o", "200o", "210o", "210s", "030o", "031o"]
GROUPS_3 = [("032", [["010o", "300o", "110o", "200o", "210o"]]), ("210", [["030o", "031o"]])]


def offset(name):
    return tuple(int(t) for t in name[:3])


def fetch(block, distance, flip=False):
    dx, dy, dz = distance
    pairs = []
    for z, low, high, x, core in itertools.product(range(4), range(2), range(2), range(4), range(2)):
        y = (2 * high + low + dy) % 4
        source = ((((z + dz) % 4 * 2 + y % 2) * 2 + y // 2) * 4 + (x + dx) % 4) * 2 + (core ^ int(flip))
        target = (((z * 2 + low) * 2 + high) * 4 + x) * 2 + core
        pairs.append((source, target))
    return lax.ppermute(block, ("chip", "core"), pairs)


def swap(block):
    return fetch(block, (0, 0, 0), True)


def sibling(block):
    both = lax.all_gather(block, "core", axis=0, tiled=True)
    return lax.dynamic_slice_in_dim(both, (1 - lax.axis_index("core")) * ROWS, ROWS)


def give(block, name):
    return fetch(block, tuple(-t for t in offset(name)), name[3] == "s")


def unit_kernel(student, teacher, out):
    for source, first, width in ((student, 0, DS), (teacher, DS, DT)):
        wide = source[...].astype(jnp.float32)
        recip = 1.0 / jnp.sqrt(jnp.sum(wide * wide, axis=1, keepdims=True) + 1e-06)
        out[:, first : first + width] = (wide * recip).astype(jnp.bfloat16)


def unit_rows(student, teacher):
    return pl.pallas_call(
        unit_kernel,
        out_shape=jax.ShapeDtypeStruct((ROWS, WIDE), jnp.bfloat16),
        in_specs=[pl.BlockSpec(memory_space=pltpu.VMEM)] * 2,
        out_specs=pl.BlockSpec(memory_space=pltpu.VMEM),
        compiler_params=pltpu.CompilerParams(vmem_limit_bytes=16 << 20),
        name="unit_rows",
    )(student, teacher)


def involution(one, two):
    return all((2 * (s - t)) % 4 == 0 for s, t in zip(offset(one), offset(two)))


def phase_kernel(layout, groups, pieces, starts, adds, outs, *refs):
    at = {name: i * ROWS for i, name in enumerate(layout)}
    refs = list(refs)
    block_refs = [refs.pop(0) for _ in pieces]
    start_refs = [refs.pop(0) for _ in starts]
    add_ref = refs.pop(0) if adds else None
    out_refs = [refs.pop(0) for _ in outs]
    sums, weight = refs
    blocks = {}
    for (name, first), ref in zip(pieces, block_refs):
        blocks.setdefault(name, []).append((first, ref))
    so_far = {}
    for names, ref in zip(starts, start_refs):
        for i, name in enumerate(names):
            so_far[name] = ref.at[pl.ds(i * ROWS, ROWS), :]

    def read(names, first, width):
        rows = []
        for name in names:
            parts = []
            for start, ref in sorted(blocks[name], key=lambda item: item[0]):
                low, high = max(first, start), min(first + width, start + ref.shape[1])
                if low < high:
                    parts.append(ref[:, low - start : high - start])
            rows.append(parts[0] if len(parts) == 1 else jnp.concatenate(parts, axis=1))
        return rows[0] if len(rows) == 1 else jnp.concatenate(rows, axis=0)

    touched = set()

    def put(names, value):
        for i, name in enumerate(names):
            rows = pl.ds(at[name], ROWS)
            part = value[i * ROWS : (i + 1) * ROWS]
            if name in touched:
                sums[rows, :] += part
            elif name in so_far:
                sums[rows, :] = part + so_far[name][...]
            else:
                sums[rows, :] = part
            touched.add(name)

    nt = (((1,), (1,)), ((), ()))
    tn = (((0,), (0,)), ((), ()))
    halves = [sorted([a + "o", a + "s"], key=at.get) for a, _ in groups]
    for number, (a, runs) in enumerate(groups):
        both = halves[number]
        columns = pl.ds(number * 2 * ROWS, 2 * ROWS)
        for run in runs:
            for i in range(0, len(run), PM):
                piece = run[i : i + PM]
                gram_s = lax.dot_general(
                    read(piece, 0, DS), read(both, 0, DS), nt, preferred_element_type=jnp.float32
                )
                gram_t = lax.dot_general(
                    read(piece, DS, DT), read(both, DS, DT), nt, preferred_element_type=jnp.float32
                )
                for j, name in enumerate(piece):
                    squash_s = jnp.tanh(SCALE_S * gram_s[j * ROWS : (j + 1) * ROWS])
                    squash_t = jnp.tanh(SCALE_T * gram_t[j * ROWS : (j + 1) * ROWS])
                    value = (squash_s - squash_t) * SCALE_S * (1.0 - squash_s * squash_s)
                    if name[:3] != a and involution(a, name):
                        value = 0.5 * value
                    weight[pl.ds(at[name], ROWS), columns] = value.astype(jnp.bfloat16)
            if run[0][:3] != a:
                put(both, lax.dot_general(
                    weight[pl.ds(at[run[0]], len(run) * ROWS), columns], read(run, 0, DS), tn,
                    preferred_element_type=jnp.float32,
                ))
    met = {}
    for number, (a, runs) in enumerate(groups):
        for run in runs:
            for name in run:
                met.setdefault(name, []).append(number)
    merged = []
    for name in sorted(met, key=at.get):
        if merged and met[merged[-1][-1]] == met[name] and at[merged[-1][-1]] + ROWS == at[name]:
            merged[-1].append(name)
        else:
            merged.append([name])
    for run in merged:
        first, last = met[run[0]][0], met[run[0]][-1] + 1
        put(run, jnp.dot(
            weight[pl.ds(at[run[0]], len(run) * ROWS), pl.ds(first * 2 * ROWS, (last - first) * 2 * ROWS)],
            read(sum(halves[first:last], []), 0, DS), preferred_element_type=jnp.float32,
        ))
    for names, ref in zip(outs, out_refs):
        for i, name in enumerate(names):
            value = sums[pl.ds(at[name], ROWS), :] if name in touched else so_far[name][...]
            if name in adds:
                value = value + add_ref[pl.ds(adds.index(name) * ROWS, ROWS), :].astype(jnp.float32)
            ref[pl.ds(i * ROWS, ROWS), :] = value.astype(ref.dtype)


def phase(name, layout, groups, blocks, starts, adds, outs):
    pairs = sum(len(run) for _, runs in groups for run in runs)
    shapes = [jax.ShapeDtypeStruct((len(names) * ROWS, DS), kind) for names, kind in outs]
    operands = [array for _, _, array in blocks] + [array for _, array in starts]
    if adds:
        operands.append(adds[1])
    return pl.pallas_call(
        functools.partial(
            phase_kernel, layout, groups, [(n, f) for n, f, _ in blocks], [names for names, _ in starts],
            adds[0] if adds else [], [names for names, _ in outs],
        ),
        out_shape=shapes,
        in_specs=[pl.BlockSpec(memory_space=pltpu.VMEM)] * len(operands),
        out_specs=[pl.BlockSpec(memory_space=pltpu.VMEM)] * len(shapes),
        scratch_shapes=[
            pltpu.VMEM((len(layout) * ROWS, DS), jnp.float32),
            pltpu.VMEM((len(layout) * ROWS, len(groups) * 2 * ROWS), jnp.bfloat16),
        ],
        compiler_params=pltpu.CompilerParams(vmem_limit_bytes=20 << 20),
        cost_estimate=pl.CostEstimate(
            flops=pairs * 2 * ROWS * 2 * ROWS * (WIDE + 2 * DS) * 2,
            bytes_accessed=sum(x.size * x.dtype.itemsize for x in operands), transcendentals=0,
        ),
        name=name,
    )(*operands)


def after(value, *others):
    return lax.optimization_barrier((value, *others))[0]


def local(student, teacher):
    own = unit_rows(student, teacher)
    f32, bf16 = jnp.float32, jnp.bfloat16
    got = {"000o": own, "000s": sibling(own)}
    for name in ("010o", "300o", "030o", "003o", "001o"):
        got[name] = fetch(own, offset(name))
    for a in ("010", "300"):
        got[a + "s"] = swap(after(got[a + "o"], got["001o"], got["000s"]))
    got["110o"] = fetch(got["010o"], (1, 0, 0))
    got["200o"] = fetch(got["300o"], (3, 0, 0))
    got["031o"] = fetch(got["030o"], (0, 0, 1))
    middle = after(got["003o"], got["010s"], got["300s"])
    got["033o"] = fetch(middle, (0, 3, 0))
    got["002o"] = fetch(middle, (0, 0, 3))

    rows = lambda layout: [(name, 0, got[name]) for name in layout if name in got]
    names_1 = ["000s", "000o", "001o", "003o", "030o", "300o", "300s", "010o", "010s"]
    (sums_1,) = phase("phase_1", LAYOUT_1, GROUPS_1, rows(LAYOUT_1), [], None, [(names_1, f32)])

    got, sums_1 = lax.optimization_barrier((got, sums_1))
    for a in ("110", "200"):
        got[a + "s"] = swap(got[a + "o"])
    late = {
        ("210o", HALF): fetch(got["110o"][:, HALF:], (1, 0, 0)),
        ("210o", 0): fetch(got["200o"][:, :HALF], (0, 1, 0)),
        ("032o", 0): fetch(got["031o"][:, :HALF], (0, 0, 1)),
        ("032o", HALF): fetch(after(got["033o"], got["110s"], got["200s"])[:, HALF:], (0, 0, 3)),
    }
    names_s = ["000s", "010s", "300s", "110s", "200s"]
    names_2 = ["010o", "300o", "110o", "200o", "030o", "031o"]
    early = ["001o", "003o", "033o", "002o"]
    siblings, sums_2, home, *done = phase(
        "phase_2", LAYOUT_2, GROUPS_2, rows(LAYOUT_2), [(names_1, sums_1)], None,
        [(names_s, bf16), (names_2, f32), (["000o"], f32)] + [([name], bf16) for name in early],
    )
    *arrays, siblings, sums_2, home = lax.optimization_barrier((*late.values(), siblings, sums_2, home))
    late = dict(zip(late, arrays))
    for (name, first), array in list(late.items()):
        late[name[:3] + "s", first] = swap(array)
    siblings = swap(siblings)
    back = [give(value, name) for name, value in zip(early, done)]

    near = ["010o", "300o", "030o", "200o"]
    crossing, sum_032, sum_210, sum_031, sum_110, *done = phase(
        "phase_3", LAYOUT_3, GROUPS_3, rows(LAYOUT_3) + [(name, first, array) for (name, first), array in late.items()],
        [(names_2, sums_2)], (["none", "010o", "300o", "110o", "200o"], siblings),
        [(["032s", "210s"], bf16)] + [([name], f32) for name in ("032o", "210o", "031o", "110o")]
        + [([name], bf16) for name in near],
    )
    crossing, back[0], back[1] = lax.optimization_barrier((crossing, back[0], back[1]))
    crossing = swap(crossing).astype(f32)
    to_031 = fetch((sum_032 + crossing[:ROWS]).astype(bf16), (0, 0, 3))
    to_110 = fetch((sum_210 + crossing[ROWS:]).astype(bf16), (3, 0, 0))
    back += [give(value, name) for name, value in zip(near, done)]
    back.append(give((sum_031 + to_031.astype(f32)).astype(bf16), "031o"))
    back.append(give((sum_110 + to_110.astype(f32)).astype(bf16), "110o"))

    summed = home + siblings[:ROWS].astype(f32)
    for value in back:
        summed = summed + value.astype(f32)
    wide = student.astype(f32)
    recip = 1.0 / jnp.sqrt(jnp.sum(wide * wide, axis=1, keepdims=True) + 1e-06)
    unit_f = wide * recip
    dunit = (4.0 * DS / math.sqrt(16384)) * summed
    inner = jnp.sum(dunit * unit_f, axis=1, keepdims=True)
    return recip * (dunit - inner * unit_f)


def solution(mesh):
    cores = jax.sharding.Mesh(mesh.devices.reshape(-1, 2), ("chip", "core"))
    spec = P(("chip", "core"), None)
    return jax.shard_map(local, mesh=cores, in_specs=(spec, spec), out_specs=spec, check_vma=False)
```

```python
import functools
import itertools
import math

import jax
import jax.numpy as jnp
from jax import lax
from jax.experimental import pallas as pl
from jax.experimental.pallas import tpu as pltpu
from jax.sharding import PartitionSpec as P

ROWS = 128
DS, DT = 1024, 4096
WIDE = DS + DT
HALF = WIDE // 2
PM = 2
SCALE_S, SCALE_T = math.sqrt(DS), math.sqrt(DT)

LAYOUT_1 = ["000s", "000o", "001o", "003o", "030o", "300o", "300s", "010o", "010s"]
GROUPS_1 = [("000", [["000o"], ["001o"]]), ("300", [["000o", "001o", "003o", "030o"]]),
            ("010", [["000o", "001o", "003o", "030o", "300o"]])]
LAYOUT_2 = ["000s", "000o", "010o", "010s", "300o", "300s", "200o", "200s",
            "030o", "003o", "001o", "002o", "031o", "033o", "110o", "110s"]
GROUPS_2 = [("000", [["002o"], ["200o"]]), ("010", [["002o", "031o"]]), ("300", [["002o", "031o", "033o", "110o"]]),
            ("200", [["001o", "002o", "031o", "033o"]]), ("110", [["030o", "003o", "001o", "002o", "031o", "033o"]])]
LAYOUT_3 = ["032o", "032s", "010o", "300o", "110o", "200o", "210o", "210s", "030o", "031o"]
GROUPS_3 = [("032", [["010o", "300o", "110o", "200o", "210o"]]), ("210", [["030o", "031o"]])]


def offset(name):
    return tuple(int(t) for t in name[:3])


def fetch(block, distance, flip=False):
    dx, dy, dz = distance
    pairs = []
    for z, low, high, x, core in itertools.product(range(4), range(2), range(2), range(4), range(2)):
        y = (2 * high + low + dy) % 4
        source = ((((z + dz) % 4 * 2 + y % 2) * 2 + y // 2) * 4 + (x + dx) % 4) * 2 + (core ^ int(flip))
        target = (((z * 2 + low) * 2 + high) * 4 + x) * 2 + core
        pairs.append((source, target))
    return lax.ppermute(block, ("chip", "core"), pairs)


def swap(block):
    return fetch(block, (0, 0, 0), True)


def give(block, name):
    return fetch(block, tuple(-t for t in offset(name)), name[3] == "s")


def unit_kernel(student, teacher, out, held_s, held_t, sems):
    parts = [(student, held_s, 0, i * 32) for i in range(4)] + [(teacher, held_t, DS, i * 32) for i in range(4)]
    copies = []
    for i, (source, held, _, row) in enumerate(parts):
        copies.append(pltpu.make_async_copy(source.at[pl.ds(row, 32), :], held.at[pl.ds(row, 32), :], sems.at[i]))
        copies[-1].start()
    for copy, (_, held, first, row) in zip(copies, parts):
        copy.wait()
        wide = held[pl.ds(row, 32), :].astype(jnp.float32)
        recip = 1.0 / jnp.sqrt(jnp.sum(wide * wide, axis=1, keepdims=True) + 1e-06)
        out[pl.ds(row, 32), first : first + held.shape[1]] = (wide * recip).astype(jnp.bfloat16)


def unit_rows(student, teacher):
    return pl.pallas_call(
        unit_kernel,
        out_shape=jax.ShapeDtypeStruct((ROWS, WIDE), jnp.bfloat16),
        in_specs=[pl.BlockSpec(memory_space=pl.ANY)] * 2,
        out_specs=pl.BlockSpec(memory_space=pltpu.VMEM),
        scratch_shapes=[
            pltpu.VMEM((ROWS, DS), jnp.bfloat16), pltpu.VMEM((ROWS, DT), jnp.bfloat16), pltpu.SemaphoreType.DMA((8,)),
        ],
        compiler_params=pltpu.CompilerParams(vmem_limit_bytes=62 << 20),
        name="unit_rows",
    )(student, teacher)


def involution(one, two):
    return all((2 * (s - t)) % 4 == 0 for s, t in zip(offset(one), offset(two)))


def phase_kernel(layout, groups, pieces, starts, adds, outs, *refs):
    at = {name: i * ROWS for i, name in enumerate(layout)}
    refs = list(refs)
    block_refs = [refs.pop(0) for _ in pieces]
    start_refs = [refs.pop(0) for _ in starts]
    add_ref = refs.pop(0) if adds else None
    out_refs = [refs.pop(0) for _ in outs]
    sums, weight = refs
    blocks = {}
    for (name, first), ref in zip(pieces, block_refs):
        blocks.setdefault(name, []).append((first, ref))
    so_far = {}
    for names, ref in zip(starts, start_refs):
        for i, name in enumerate(names):
            so_far[name] = ref.at[pl.ds(i * ROWS, ROWS), :]

    def read(names, first, width):
        rows = []
        for name in names:
            parts = []
            for start, ref in sorted(blocks[name], key=lambda item: item[0]):
                low, high = max(first, start), min(first + width, start + ref.shape[1])
                if low < high:
                    parts.append(ref[:, low - start : high - start])
            rows.append(parts[0] if len(parts) == 1 else jnp.concatenate(parts, axis=1))
        return rows[0] if len(rows) == 1 else jnp.concatenate(rows, axis=0)

    touched = set()

    def put(names, value):
        for i, name in enumerate(names):
            rows = pl.ds(at[name], ROWS)
            part = value[i * ROWS : (i + 1) * ROWS]
            if name in touched:
                sums[rows, :] += part
            elif name in so_far:
                sums[rows, :] = part + so_far[name][...]
            else:
                sums[rows, :] = part
            touched.add(name)

    nt = (((1,), (1,)), ((), ()))
    tn = (((0,), (0,)), ((), ()))
    halves = [sorted([a + "o", a + "s"], key=at.get) for a, _ in groups]
    for number, (a, runs) in enumerate(groups):
        both = halves[number]
        columns = pl.ds(number * 2 * ROWS, 2 * ROWS)
        for run in runs:
            for i in range(0, len(run), PM):
                piece = run[i : i + PM]
                gram_s = lax.dot_general(
                    read(piece, 0, DS), read(both, 0, DS), nt, preferred_element_type=jnp.float32
                )
                gram_t = lax.dot_general(
                    read(piece, DS, DT), read(both, DS, DT), nt, preferred_element_type=jnp.float32
                )
                for j, name in enumerate(piece):
                    squash_s = jnp.tanh(SCALE_S * gram_s[j * ROWS : (j + 1) * ROWS])
                    squash_t = jnp.tanh(SCALE_T * gram_t[j * ROWS : (j + 1) * ROWS])
                    value = (squash_s - squash_t) * SCALE_S * (1.0 - squash_s * squash_s)
                    if name[:3] != a and involution(a, name):
                        value = 0.5 * value
                    weight[pl.ds(at[name], ROWS), columns] = value.astype(jnp.bfloat16)
            if run[0][:3] != a:
                put(both, lax.dot_general(
                    weight[pl.ds(at[run[0]], len(run) * ROWS), columns], read(run, 0, DS), tn,
                    preferred_element_type=jnp.float32,
                ))
    met = {}
    for number, (a, runs) in enumerate(groups):
        for run in runs:
            for name in run:
                met.setdefault(name, []).append(number)
    merged = []
    for name in sorted(met, key=at.get):
        if merged and met[merged[-1][-1]] == met[name] and at[merged[-1][-1]] + ROWS == at[name]:
            merged[-1].append(name)
        else:
            merged.append([name])
    for run in merged:
        first, last = met[run[0]][0], met[run[0]][-1] + 1
        put(run, jnp.dot(
            weight[pl.ds(at[run[0]], len(run) * ROWS), pl.ds(first * 2 * ROWS, (last - first) * 2 * ROWS)],
            read(sum(halves[first:last], []), 0, DS), preferred_element_type=jnp.float32,
        ))
    for names, ref in zip(outs, out_refs):
        for i, name in enumerate(names):
            value = sums[pl.ds(at[name], ROWS), :] if name in touched else so_far[name][...]
            if name in adds:
                value = value + add_ref[pl.ds(adds.index(name) * ROWS, ROWS), :].astype(jnp.float32)
            ref[pl.ds(i * ROWS, ROWS), :] = value.astype(ref.dtype)


def phase(name, layout, groups, blocks, starts, adds, outs):
    pairs = sum(len(run) for _, runs in groups for run in runs)
    shapes = [jax.ShapeDtypeStruct((len(names) * ROWS, DS), kind) for names, kind in outs]
    operands = [array for _, _, array in blocks] + [array for _, array in starts]
    if adds:
        operands.append(adds[1])
    return pl.pallas_call(
        functools.partial(
            phase_kernel, layout, groups, [(n, f) for n, f, _ in blocks], [names for names, _ in starts],
            adds[0] if adds else [], [names for names, _ in outs],
        ),
        out_shape=shapes,
        in_specs=[pl.BlockSpec(memory_space=pltpu.VMEM)] * len(operands),
        out_specs=[pl.BlockSpec(memory_space=pltpu.VMEM)] * len(shapes),
        scratch_shapes=[
            pltpu.VMEM((len(layout) * ROWS, DS), jnp.float32),
            pltpu.VMEM((len(layout) * ROWS, len(groups) * 2 * ROWS), jnp.bfloat16),
        ],
        compiler_params=pltpu.CompilerParams(vmem_limit_bytes=20 << 20),
        cost_estimate=pl.CostEstimate(
            flops=pairs * 2 * ROWS * 2 * ROWS * (WIDE + 2 * DS) * 2,
            bytes_accessed=sum(x.size * x.dtype.itemsize for x in operands), transcendentals=0,
        ),
        name=name,
    )(*operands)


def after(value, *others):
    return lax.optimization_barrier((value, *others))[0]


def local(student, teacher):
    own = unit_rows(student, teacher)
    f32, bf16 = jnp.float32, jnp.bfloat16
    got = {"000o": own, "000s": swap(own)}
    for name in ("010o", "300o", "030o", "003o"):
        got[name] = fetch(own, offset(name))
    got["001o"] = fetch(after(own, got["000s"]), (0, 0, 1))
    for a in ("010", "300"):
        got[a + "s"] = swap(after(got[a + "o"], got["001o"]))
    got["110o"] = fetch(got["010o"], (1, 0, 0))
    got["200o"] = fetch(got["300o"], (3, 0, 0))
    got["031o"] = fetch(got["030o"], (0, 0, 1))
    middle = after(got["003o"], got["010s"], got["300s"])
    got["033o"] = fetch(middle, (0, 3, 0))
    got["002o"] = fetch(middle, (0, 0, 3))

    rows = lambda layout: [(name, 0, got[name]) for name in layout if name in got]
    names_1 = ["000s", "000o", "001o", "003o", "030o", "300o", "300s", "010o", "010s"]
    (sums_1,) = phase("phase_1", LAYOUT_1, GROUPS_1, rows(LAYOUT_1), [], None, [(names_1, f32)])

    got, sums_1 = lax.optimization_barrier((got, sums_1))
    for a in ("110", "200"):
        got[a + "s"] = swap(got[a + "o"])
    late = {
        ("210o", HALF): fetch(got["110o"][:, HALF:], (1, 0, 0)),
        ("210o", 0): fetch(got["200o"][:, :HALF], (0, 1, 0)),
        ("032o", 0): fetch(got["031o"][:, :HALF], (0, 0, 1)),
        ("032o", HALF): fetch(after(got["033o"], got["110s"], got["200s"])[:, HALF:], (0, 0, 3)),
    }
    names_s = ["000s", "010s", "300s", "110s", "200s"]
    names_2 = ["010o", "300o", "110o", "200o", "030o", "031o"]
    early = ["001o", "003o", "033o", "002o"]
    siblings, sums_2, home, *done = phase(
        "phase_2", LAYOUT_2, GROUPS_2, rows(LAYOUT_2), [(names_1, sums_1)], None,
        [(names_s, bf16), (names_2, f32), (["000o"], f32)] + [([name], bf16) for name in early],
    )
    *arrays, siblings, sums_2 = lax.optimization_barrier((*late.values(), siblings, sums_2))
    late = dict(zip(late, arrays))
    for (name, first), array in list(late.items()):
        late[name[:3] + "s", first] = swap(array)
    siblings = swap(after(siblings, *late.values()))
    back = [give(value, name) for name, value in zip(early, done)]

    near = ["010o", "300o", "030o", "200o"]
    crossing, *done = phase(
        "phase_3", LAYOUT_3, GROUPS_3, rows(LAYOUT_3) + [(name, first, array) for (name, first), array in late.items()],
        [(names_2, sums_2)], None,
        [(["032s", "210s"], bf16)] + [([name], f32) for name in ["032o", "210o", "031o", "110o"] + near],
    )
    sums = dict(zip(["032o", "210o", "031o", "110o"] + near, done))
    crossing, siblings, back[0], back[1] = lax.optimization_barrier((crossing, siblings, back[0], back[1]))
    crossing = swap(crossing).astype(f32)
    for i, name in enumerate(names_s):
        if name[:3] + "o" in sums:
            sums[name[:3] + "o"] += siblings[i * ROWS : (i + 1) * ROWS].astype(f32)
    to_031 = fetch((sums["032o"] + crossing[:ROWS]).astype(bf16), (0, 0, 3))
    to_110 = fetch((sums["210o"] + crossing[ROWS:]).astype(bf16), (3, 0, 0))
    send_031 = (sums["031o"] + to_031.astype(f32)).astype(bf16)
    send_110 = (sums["110o"] + to_110.astype(f32)).astype(bf16)
    back += [give(send_031, "031o"), give(send_110, "110o"), give(sums["030o"].astype(bf16), "030o")]
    back += [give(after(sums[name].astype(bf16), send_031, send_110), name) for name in ("010o", "300o", "200o")]

    summed = home + siblings[:ROWS].astype(f32)
    for value in back:
        summed = summed + value.astype(f32)
    wide = student.astype(f32)
    recip = 1.0 / jnp.sqrt(jnp.sum(wide * wide, axis=1, keepdims=True) + 1e-06)
    unit_f = wide * recip
    dunit = (4.0 * DS / math.sqrt(16384)) * summed
    inner = jnp.sum(dunit * unit_f, axis=1, keepdims=True)
    return recip * (dunit - inner * unit_f)


def solution(mesh):
    cores = jax.sharding.Mesh(mesh.devices.reshape(-1, 2), ("chip", "core"))
    spec = P(("chip", "core"), None)
    return jax.shard_map(local, mesh=cores, in_specs=(spec, spec), out_specs=spec, check_vma=False)
```

```python
import functools
import itertools
import math

import jax
import jax.numpy as jnp
from jax import lax
from jax.experimental import pallas as pl
from jax.experimental.pallas import tpu as pltpu
from jax.sharding import PartitionSpec as P

ROWS = 128
DS, DT = 1024, 4096
WIDE = DS + DT
HALF = WIDE // 2
PM = 2
SCALE_S, SCALE_T = math.sqrt(DS), math.sqrt(DT)

LAYOUT_1 = ["000s", "000o", "001o", "003o", "030o", "300o", "300s", "010o", "010s"]
GROUPS_1 = [("000", [["000o"], ["001o"]]), ("300", [["000o", "001o", "003o", "030o"]]),
            ("010", [["000o", "001o", "003o", "030o", "300o"]])]
LAYOUT_2 = ["000s", "000o", "010o", "010s", "300o", "300s", "200o", "200s",
            "030o", "003o", "001o", "002o", "031o", "033o", "110o", "110s"]
GROUPS_2 = [("000", [["002o"], ["200o"]]), ("010", [["002o", "031o"]]), ("300", [["002o", "031o", "033o", "110o"]]),
            ("200", [["001o", "002o", "031o", "033o"]]), ("110", [["030o", "003o", "001o", "002o", "031o", "033o"]])]
LAYOUT_3 = ["032o", "032s", "010o", "300o", "110o", "200o", "210o", "210s", "030o", "031o"]
GROUPS_3 = [("032", [["010o", "300o", "110o", "200o", "210o"]]), ("210", [["030o", "031o"]])]


def offset(name):
    return tuple(int(t) for t in name[:3])


def fetch(block, distance, flip=False):
    dx, dy, dz = distance
    pairs = []
    for z, low, high, x, core in itertools.product(range(4), range(2), range(2), range(4), range(2)):
        y = (2 * high + low + dy) % 4
        source = ((((z + dz) % 4 * 2 + y % 2) * 2 + y // 2) * 4 + (x + dx) % 4) * 2 + (core ^ int(flip))
        target = (((z * 2 + low) * 2 + high) * 4 + x) * 2 + core
        pairs.append((source, target))
    return lax.ppermute(block, ("chip", "core"), pairs)


def swap(block):
    return fetch(block, (0, 0, 0), True)


def give(block, name):
    return fetch(block, tuple(-t for t in offset(name)), name[3] == "s")


def unit_kernel(student, teacher, out, held_s, held_t, sems):
    parts = [(student, held_s, 0, i * 32) for i in range(4)] + [(teacher, held_t, DS, i * 32) for i in range(4)]
    copies = []
    for i, (source, held, _, row) in enumerate(parts):
        copies.append(pltpu.make_async_copy(source.at[pl.ds(row, 32), :], held.at[pl.ds(row, 32), :], sems.at[i]))
        copies[-1].start()
    for copy, (_, held, first, row) in zip(copies, parts):
        copy.wait()
        wide = held[pl.ds(row, 32), :].astype(jnp.float32)
        recip = 1.0 / jnp.sqrt(jnp.sum(wide * wide, axis=1, keepdims=True) + 1e-06)
        out[pl.ds(row, 32), first : first + held.shape[1]] = (wide * recip).astype(jnp.bfloat16)


def unit_rows(student, teacher):
    return pl.pallas_call(
        unit_kernel,
        out_shape=jax.ShapeDtypeStruct((ROWS, WIDE), jnp.bfloat16),
        in_specs=[pl.BlockSpec(memory_space=pl.ANY)] * 2,
        out_specs=pl.BlockSpec(memory_space=pltpu.VMEM),
        scratch_shapes=[
            pltpu.VMEM((ROWS, DS), jnp.bfloat16), pltpu.VMEM((ROWS, DT), jnp.bfloat16), pltpu.SemaphoreType.DMA((8,)),
        ],
        compiler_params=pltpu.CompilerParams(vmem_limit_bytes=62 << 20),
        name="unit_rows",
    )(student, teacher)


def involution(one, two):
    return all((2 * (s - t)) % 4 == 0 for s, t in zip(offset(one), offset(two)))


def phase_kernel(layout, groups, pieces, starts, adds, outs, *refs):
    at = {name: i * ROWS for i, name in enumerate(layout)}
    refs = list(refs)
    block_refs = [refs.pop(0) for _ in pieces]
    start_refs = [refs.pop(0) for _ in starts]
    add_ref = refs.pop(0) if adds else None
    out_refs = [refs.pop(0) for _ in outs]
    sums, weight = refs
    blocks = {}
    for (name, first), ref in zip(pieces, block_refs):
        blocks.setdefault(name, []).append((first, ref))
    so_far = {}
    for names, ref in zip(starts, start_refs):
        for i, name in enumerate(names):
            so_far[name] = ref.at[pl.ds(i * ROWS, ROWS), :]

    def read(names, first, width):
        rows = []
        for name in names:
            parts = []
            for start, ref in sorted(blocks[name], key=lambda item: item[0]):
                low, high = max(first, start), min(first + width, start + ref.shape[1])
                if low < high:
                    parts.append(ref[:, low - start : high - start])
            rows.append(parts[0] if len(parts) == 1 else jnp.concatenate(parts, axis=1))
        return rows[0] if len(rows) == 1 else jnp.concatenate(rows, axis=0)

    touched = set()

    def put(names, value):
        for i, name in enumerate(names):
            rows = pl.ds(at[name], ROWS)
            part = value[i * ROWS : (i + 1) * ROWS]
            if name in touched:
                sums[rows, :] += part
            elif name in so_far:
                sums[rows, :] = part + so_far[name][...]
            else:
                sums[rows, :] = part
            touched.add(name)

    nt = (((1,), (1,)), ((), ()))
    tn = (((0,), (0,)), ((), ()))
    halves = [sorted([a + "o", a + "s"], key=at.get) for a, _ in groups]
    for number, (a, runs) in enumerate(groups):
        both = halves[number]
        columns = pl.ds(number * 2 * ROWS, 2 * ROWS)
        for run in runs:
            for i in range(0, len(run), PM):
                piece = run[i : i + PM]
                gram_s = lax.dot_general(
                    read(piece, 0, DS), read(both, 0, DS), nt, preferred_element_type=jnp.float32
                )
                gram_t = lax.dot_general(
                    read(piece, DS, DT), read(both, DS, DT), nt, preferred_element_type=jnp.float32
                )
                for j, name in enumerate(piece):
                    squash_s = jnp.tanh(SCALE_S * gram_s[j * ROWS : (j + 1) * ROWS])
                    squash_t = jnp.tanh(SCALE_T * gram_t[j * ROWS : (j + 1) * ROWS])
                    value = (squash_s - squash_t) * SCALE_S * (1.0 - squash_s * squash_s)
                    if name[:3] != a and involution(a, name):
                        value = 0.5 * value
                    weight[pl.ds(at[name], ROWS), columns] = value.astype(jnp.bfloat16)
            if run[0][:3] != a:
                put(both, lax.dot_general(
                    weight[pl.ds(at[run[0]], len(run) * ROWS), columns], read(run, 0, DS), tn,
                    preferred_element_type=jnp.float32,
                ))
    met = {}
    for number, (a, runs) in enumerate(groups):
        for run in runs:
            for name in run:
                met.setdefault(name, []).append(number)
    merged = []
    for name in sorted(met, key=at.get):
        if merged and met[merged[-1][-1]] == met[name] and at[merged[-1][-1]] + ROWS == at[name]:
            merged[-1].append(name)
        else:
            merged.append([name])
    for run in merged:
        first, last = met[run[0]][0], met[run[0]][-1] + 1
        put(run, jnp.dot(
            weight[pl.ds(at[run[0]], len(run) * ROWS), pl.ds(first * 2 * ROWS, (last - first) * 2 * ROWS)],
            read(sum(halves[first:last], []), 0, DS), preferred_element_type=jnp.float32,
        ))
    for names, ref in zip(outs, out_refs):
        for i, name in enumerate(names):
            value = sums[pl.ds(at[name], ROWS), :] if name in touched else so_far[name][...]
            if name in adds:
                value = value + add_ref[pl.ds(adds.index(name) * ROWS, ROWS), :].astype(jnp.float32)
            ref[pl.ds(i * ROWS, ROWS), :] = value.astype(ref.dtype)


def phase(name, layout, groups, blocks, starts, adds, outs):
    pairs = sum(len(run) for _, runs in groups for run in runs)
    shapes = [jax.ShapeDtypeStruct((len(names) * ROWS, DS), kind) for names, kind in outs]
    operands = [array for _, _, array in blocks] + [array for _, array in starts]
    if adds:
        operands.append(adds[1])
    return pl.pallas_call(
        functools.partial(
            phase_kernel, layout, groups, [(n, f) for n, f, _ in blocks], [names for names, _ in starts],
            adds[0] if adds else [], [names for names, _ in outs],
        ),
        out_shape=shapes,
        in_specs=[pl.BlockSpec(memory_space=pltpu.VMEM)] * len(operands),
        out_specs=[pl.BlockSpec(memory_space=pltpu.VMEM)] * len(shapes),
        scratch_shapes=[
            pltpu.VMEM((len(layout) * ROWS, DS), jnp.float32),
            pltpu.VMEM((len(layout) * ROWS, len(groups) * 2 * ROWS), jnp.bfloat16),
        ],
        compiler_params=pltpu.CompilerParams(vmem_limit_bytes=20 << 20),
        cost_estimate=pl.CostEstimate(
            flops=pairs * 2 * ROWS * 2 * ROWS * (WIDE + 2 * DS) * 2,
            bytes_accessed=sum(x.size * x.dtype.itemsize for x in operands), transcendentals=0,
        ),
        name=name,
    )(*operands)


def after(value, *others):
    return lax.optimization_barrier((value, *others))[0]


def local(student, teacher):
    own = unit_rows(student, teacher)
    f32, bf16 = jnp.float32, jnp.bfloat16
    got = {"000o": own, "000s": swap(own)}
    for name in ("010o", "300o", "030o", "003o"):
        got[name] = fetch(own, offset(name))
    got["001o"] = fetch(after(own, got["000s"]), (0, 0, 1))
    for a in ("010", "300"):
        got[a + "s"] = swap(after(got[a + "o"], got["001o"]))
    got["110o"] = fetch(got["010o"], (1, 0, 0))
    got["200o"] = fetch(got["300o"], (3, 0, 0))
    got["031o"] = fetch(got["030o"], (0, 0, 1))
    middle = after(got["003o"], got["010s"], got["300s"])
    got["033o"] = fetch(middle, (0, 3, 0))
    got["002o"] = fetch(middle, (0, 0, 3))

    rows = lambda layout: [(name, 0, got[name]) for name in layout if name in got]
    names_1 = ["000s", "000o", "001o", "003o", "030o", "300o", "300s", "010o", "010s"]
    (sums_1,) = phase("phase_1", LAYOUT_1, GROUPS_1, rows(LAYOUT_1), [], None, [(names_1, f32)])

    got, sums_1 = lax.optimization_barrier((got, sums_1))
    for a in ("110", "200"):
        got[a + "s"] = swap(got[a + "o"])
    late = {
        ("210o", HALF): fetch(got["110o"][:, HALF:], (1, 0, 0)),
        ("210o", 0): fetch(got["200o"][:, :HALF], (0, 1, 0)),
        ("032o", 0): fetch(got["031o"][:, :HALF], (0, 0, 1)),
        ("032o", HALF): fetch(after(got["033o"], got["110s"], got["200s"])[:, HALF:], (0, 0, 3)),
    }
    names_s = ["000s", "010s", "300s", "110s", "200s"]
    names_2 = ["010o", "300o", "110o", "200o", "030o", "031o"]
    early = ["001o", "003o", "033o", "002o"]
    siblings, sums_2, home, *done = phase(
        "phase_2", LAYOUT_2, GROUPS_2, rows(LAYOUT_2), [(names_1, sums_1)], None,
        [(names_s, bf16), (names_2, f32), (["000o"], f32)] + [([name], bf16) for name in early],
    )
    *arrays, siblings, sums_2 = lax.optimization_barrier((*late.values(), siblings, sums_2))
    late = dict(zip(late, arrays))
    for (name, first), array in list(late.items()):
        late[name[:3] + "s", first] = swap(array)
    siblings = swap(after(siblings, *late.values()))
    sum_001, outer = done[0], done[2:]
    back = [give(done[1], "003o")]

    near = ["010o", "300o", "030o", "200o"]
    crossing, *done = phase(
        "phase_3", LAYOUT_3, GROUPS_3, rows(LAYOUT_3) + [(name, first, array) for (name, first), array in late.items()],
        [(names_2, sums_2)], None,
        [(["032s", "210s"], bf16)] + [([name], f32) for name in ["032o", "210o", "031o", "110o"] + near],
    )
    sums = dict(zip(["032o", "210o", "031o", "110o"] + near, done))
    crossing, siblings = lax.optimization_barrier((crossing, siblings))
    crossing = swap(crossing).astype(f32)
    for i, name in enumerate(names_s):
        if name[:3] + "o" in sums:
            sums[name[:3] + "o"] += siblings[i * ROWS : (i + 1) * ROWS].astype(f32)
    back[0], far_032, far_210, last_110, *aside = lax.optimization_barrier((
        back[0],
        sums["032o"] + crossing[:ROWS], sums["210o"] + crossing[ROWS:],
        sums["110o"].astype(bf16), sums["300o"].astype(bf16), sums["030o"].astype(bf16),
    ))
    up = fetch(jnp.concatenate([far_032.astype(bf16), sum_001]), (0, 0, 3))
    along = fetch(jnp.concatenate([far_210, sums["010o"]]).astype(bf16), (0, 3, 0))
    back += [up[ROWS:], along[ROWS:]]
    send_031 = (sums["031o"] + up[:ROWS].astype(f32)).astype(bf16)
    send_200 = (sums["200o"] + along[:ROWS].astype(f32)).astype(bf16)
    back += [give(send_031, "031o"), give(send_200, "200o")]
    back += [give(value, name) for name, value in zip(("300o", "030o"), aside)]
    back += [give(after(value, send_031, send_200), name) for name, value in zip(["110o"] + early[2:], [last_110] + outer)]

    summed = home + siblings[:ROWS].astype(f32)
    for value in back:
        summed = summed + value.astype(f32)
    wide = student.astype(f32)
    recip = 1.0 / jnp.sqrt(jnp.sum(wide * wide, axis=1, keepdims=True) + 1e-06)
    unit_f = wide * recip
    dunit = (4.0 * DS / math.sqrt(16384)) * summed
    inner = jnp.sum(dunit * unit_f, axis=1, keepdims=True)
    return recip * (dunit - inner * unit_f)


def solution(mesh):
    cores = jax.sharding.Mesh(mesh.devices.reshape(-1, 2), ("chip", "core"))
    spec = P(("chip", "core"), None)
    return jax.shard_map(local, mesh=cores, in_specs=(spec, spec), out_specs=spec, check_vma=False)
```
